32 devices in a mesh: rows: 16 (over z, y, core), cols: 2 (over x).
Axes of the slice: x: 2, y: 2, z: 4, core: 2. Of those that a mesh axis runs over, the one named last changes fastest.
Arguments:
- lower_coupling: bfloat16 [16, 1024, 1024], P('rows', 'cols'), may hold values from -0.0625 to 0.0625
- upper_coupling: bfloat16 [16, 1024, 1024], P('rows', 'cols'), may hold values from -0.0625 to 0.0625
- solution: bfloat16 [16, 1024, 256], P('rows', None, 'cols'), may hold values from -0.375 to 0.375
- cotangent: bfloat16 [16, 1024, 256], P('rows', None, 'cols'), may hold values from -6 to 6
Outputs:
- source_grad: bfloat16 [16, 1024, 256], P('rows', None, 'cols')
- lower_grad: bfloat16 [16, 1024, 1024], P('rows', 'cols')
- upper_grad: bfloat16 [16, 1024, 1024], P('rows', 'cols')
The draws below stay inside these ranges and needn't reach their ends.
All inputs are finite; a program needn't handle non-finite values.
Results may differ from the reference program's by a relative error of at most 0.0085.
Values may be sent and summed in bfloat16 or wider, within the bound.
A program may use at most 64 MiB of HBM per device.

```python
import jax
import jax.numpy as jnp
import numpy as np
from jax import lax

BLOCK = 1024
ROWS = 16
COLUMNS = 256
LEVELS = 4


def level_of(stream_key, dims, pieces, least, high):
    gain, own = 1.0, jax.random.fold_in(stream_key, 6)
    for position, shards_of in pieces:
        draws = jnp.exp(jax.random.uniform(jax.random.fold_in(own, position), (shards_of,), jnp.float32, least / len(pieces), high / len(pieces)))
        gain = gain * jnp.repeat(draws, dims[position] // shards_of).reshape([-1 if axis == position else 1 for axis in range(len(dims))])
    return gain


def noise(stream_key, extent, spread, limit, pieces=(), dtype=jnp.bfloat16):
    array = spread * jax.random.normal(stream_key, extent, jnp.float32)
    if pieces:
        array = array * level_of(stream_key, extent, pieces, -0.22, 0.18)
    return jnp.clip(array, -limit, limit).astype(dtype)


def setup_inputs(seed: int = 0) -> dict:
    arg_keys = jax.random.split(jax.random.key(seed), 5)
    return {
        "lower_coupling": noise(arg_keys[0], (ROWS, BLOCK, BLOCK), (8 * BLOCK) ** -0.5, 0.0625, ((0, 16), (1, 2))),
        "upper_coupling": noise(arg_keys[1], (ROWS, BLOCK, BLOCK), (8 * BLOCK) ** -0.5, 0.0625, ((0, 16), (1, 2))),
        "solution": noise(arg_keys[2], (ROWS, BLOCK, COLUMNS), COLUMNS ** -0.5, 0.375, ((0, 16), (2, 2))),
        "cotangent": noise(arg_keys[3], (ROWS, BLOCK, COLUMNS), 1.0, 6.0, ((0, 16), (2, 2))),
    }


def reference(lower_coupling, upper_coupling, solution, cotangent):
    adjoint = cotangent.astype(jnp.float32)
    for level_no in range(LEVELS):
        stride = 2 ** level_no
        active = (np.arange(stride, ROWS, 2 * stride) + 1) % ROWS
        factor = adjoint[active].astype(jnp.bfloat16).astype(jnp.float32)
        push_down = jnp.einsum("kij,kir->kjr", lower_coupling[active].astype(jnp.float32), factor)
        push_up = jnp.einsum("kij,kir->kjr", upper_coupling[active].astype(jnp.float32), factor)
        push_down = lax.optimization_barrier(push_down.astype(jnp.bfloat16)).astype(jnp.float32)
        push_up = lax.optimization_barrier(push_up.astype(jnp.bfloat16)).astype(jnp.float32)
        adjoint = adjoint.at[(active - stride) % ROWS].add(-push_down)
        adjoint = adjoint.at[(active + stride) % ROWS].add(-push_up)
    source_grad = adjoint.astype(jnp.bfloat16)
    lower_grad = jnp.zeros((ROWS, BLOCK, BLOCK), jnp.bfloat16)
    upper_grad = jnp.zeros((ROWS, BLOCK, BLOCK), jnp.bfloat16)
    for level_no in range(LEVELS):
        stride = 2 ** level_no
        active = (np.arange(stride, ROWS, 2 * stride) + 1) % ROWS
        factor = source_grad[active].astype(jnp.float32)
        block_below = solution[(active - stride) % ROWS].astype(jnp.float32)
        block_above = solution[(active + stride) % ROWS].astype(jnp.float32)
        grad_low = -jnp.einsum("kbr,kcr->kbc", factor, block_below)
        grad_high = -jnp.einsum("kbr,kcr->kbc", factor, block_above)
        lower_grad = lower_grad.at[active].set(grad_low.astype(jnp.bfloat16))
        upper_grad = upper_grad.at[active].set(grad_high.astype(jnp.bfloat16))
    return (source_grad, lower_grad, upper_grad)
```

```python
import functools

import jax
import jax.numpy as jnp
from jax import lax
from jax.experimental import pallas as pl
from jax.experimental.pallas import tpu as pltpu
from jax.sharding import PartitionSpec as P

MESH = pl.DeviceIdType.MESH
F32 = jnp.float32
BF16 = jnp.bfloat16


def kernel(n, nx, lower_hbm, upper_hbm, sol_hbm, cot_hbm, src_out, low_out, up_out,
           low_v, up_v, sol_v, cot_v, cot_t, cot_half, acc, factor_t, factor, push_out,
           push_in, root_out, root_in, near, src_t, src_v, grad_v,
           load_sem, store_sem, cot_ss, cot_rs, push_ss, push_rs, root_ss, root_rs,
           sol_ss, sol_rs, near_ss, near_rs, src_ss, src_rs):
    block, width = cot_v.shape
    half = block // nx
    levels = n.bit_length() - 1
    last = levels - 1
    row = lax.axis_index("rows")
    col = lax.axis_index("cols")
    offset = lax.rem(row + n - 1, n)
    level = jnp.int32(0)
    for l in range(levels):
        level = level + jnp.where(lax.rem(offset, 2 << l) == 0, 1, 0)
    is_root = level == levels
    is_last = level == last
    stride = jnp.int32(1)
    for l in range(levels):
        stride = jnp.where(level > l, 2 << l, stride)
    stride = jnp.where(is_root, 0, stride)

    def other(k):
        return lax.rem(col + k, nx)

    def up_row(s):
        return lax.rem(row + s, n)

    def down_row(s):
        return lax.rem(row + n - s, n)

    loads = [
        pltpu.make_async_copy(cot_hbm.at[0], cot_v, load_sem.at[0]),
        pltpu.make_async_copy(lower_hbm.at[0], low_v, load_sem.at[1]),
        pltpu.make_async_copy(upper_hbm.at[0], up_v, load_sem.at[2]),
        pltpu.make_async_copy(sol_hbm.at[0], sol_v, load_sem.at[3]),
    ]
    for load in loads:
        load.start()

    barrier = pltpu.get_barrier_semaphore()
    for k in range(1, nx):
        pl.semaphore_signal(barrier, inc=1, device_id=(row, other(k)), device_id_type=MESH)
    for l in range(levels):
        @pl.when(level >= l)
        def _():
            for k in range(nx):
                pl.semaphore_signal(barrier, inc=1, device_id=(up_row(1 << l), k), device_id_type=MESH)
                if l != last:
                    pl.semaphore_signal(barrier, inc=1, device_id=(down_row(1 << l), k), device_id_type=MESH)

    loads[0].wait()
    cot_t[...] = cot_v[...].T
    low_half = pl.ds(pl.multiple_of(col * half, half), half)
    own_cols = pl.ds(pl.multiple_of(col * width, width), width)
    cot_half[own_cols, :] = cot_t[:, low_half]

    reached = jnp.minimum(level + 1, last)
    pl.semaphore_wait(barrier, (nx - 1) + nx * (2 * reached + jnp.where(level >= last, 1, 0)))

    def cot_copy(k):
        to = other(k)
        return pltpu.make_async_remote_copy(
            src_ref=cot_t.at[:, pl.ds(pl.multiple_of(to * half, half), half)],
            dst_ref=cot_half.at[own_cols, :],
            send_sem=cot_ss.at[k], recv_sem=cot_rs.at[k],
            device_id=(row, to), device_id_type=MESH)

    for k in range(1, nx):
        cot_copy(k).start()

    loads[3].wait()

    def sol_copy(l, d):
        target = up_row(1 << l) if d == 0 else down_row(1 << l)
        return pltpu.make_async_remote_copy(
            src_ref=sol_v, dst_ref=near.at[d, col],
            send_sem=sol_ss.at[l, d], recv_sem=sol_rs.at[d],
            device_id=(target, col), device_id_type=MESH)

    def each_sol(act):
        for l in range(levels):
            @pl.when(level > l)
            def _():
                for d in range(2 if l != last else 1):
                    act(sol_copy(l, d))

    each_sol(lambda c: c.start())

    def near_copy(d, k):
        return pltpu.make_async_remote_copy(
            src_ref=near.at[d, col], dst_ref=near.at[d, col],
            send_sem=near_ss.at[d, k], recv_sem=near_rs.at[d, k],
            device_id=(row, other(k)), device_id_type=MESH)

    def each_near(act):
        act(0)

        @pl.when(level < last)
        def _():
            act(1)

    def forward_near():
        def act(d):
            sol_copy(0, d).wait_recv()
            for k in range(1, nx):
                near_copy(d, k).start()
        each_near(act)

    for k in range(1, nx):
        cot_copy(k).wait_recv()
    acc[...] = cot_half[...].astype(F32)

    def push_copy(l, d, k, target):
        to = other(k)
        return pltpu.make_async_remote_copy(
            src_ref=push_out.at[d, to], dst_ref=push_in.at[l, d, col],
            send_sem=push_ss.at[d, k], recv_sem=push_rs.at[l, d, col],
            device_id=(target, to), device_id_type=MESH)

    for l in range(last):
        @pl.when(level > l)
        def _():
            for c in range(nx):
                for d in range(2):
                    pltpu.make_async_remote_copy(
                        src_ref=push_out.at[d, c], dst_ref=push_in.at[l, d, c],
                        send_sem=push_ss.at[d, c], recv_sem=push_rs.at[l, d, c],
                        device_id=(row, other(1)), device_id_type=MESH).wait_recv()
            total = push_in[l, 0, 0].astype(F32)
            for d in range(2):
                for c in range(nx):
                    if d + c:
                        total = total + push_in[l, d, c].astype(F32)
            acc[...] = acc[...] - total
            if l == 0:
                @pl.when(jnp.logical_not(is_root))
                def _():
                    forward_near()

    factor_t[...] = acc[...].astype(BF16)
    loads[1].wait()
    loads[2].wait()

    my_level = jnp.minimum(level, last - 1) if last else jnp.int32(0)

    @pl.when(level < last)
    def _():
        for k in list(range(1, nx)) + [0]:
            to = other(k)
            part = pl.ds(pl.multiple_of(to * half, half), half)
            for d, mat in ((1, low_v), (0, up_v)):
                push_out[d, to] = jnp.dot(
                    factor_t[...], mat[:, part], preferred_element_type=F32).astype(BF16)
                target = up_row(stride) if d == 0 else down_row(stride)
                push_copy(my_level, d, k, target).start()

    def root_copy(k):
        to = other(k)
        return pltpu.make_async_remote_copy(
            src_ref=root_out.at[to], dst_ref=root_in.at[col],
            send_sem=root_ss.at[k], recv_sem=root_rs.at[col],
            device_id=(up_row(1 << last), to), device_id_type=MESH)

    @pl.when(is_last)
    def _():
        for k in list(range(1, nx)) + [0]:
            to = other(k)
            rows = pl.ds(pl.multiple_of(to * width, width), width)
            both = jnp.dot(factor_t[rows, :], low_v[...], preferred_element_type=F32)
            both = both + jnp.dot(factor_t[rows, :], up_v[...], preferred_element_type=F32)
            root_out[to] = both.astype(BF16)
            root_copy(k).start()

    def src_copy(k):
        to = other(k)
        return pltpu.make_async_remote_copy(
            src_ref=factor_t.at[pl.ds(pl.multiple_of(to * width, width), width), :],
            dst_ref=src_t.at[:, low_half],
            send_sem=src_ss.at[k], recv_sem=src_rs.at[k],
            device_id=(row, to), device_id_type=MESH)

    for k in range(1, nx):
        src_copy(k).start()
    src_t[:, low_half] = factor_t[own_cols, :]

    @pl.when(level == 0)
    def _():
        forward_near()

    low_store = pltpu.make_async_copy(grad_v.at[0], low_out.at[0], store_sem.at[0])
    up_store = pltpu.make_async_copy(grad_v.at[1], up_out.at[0], store_sem.at[1])
    src_store = pltpu.make_async_copy(src_v, src_out.at[0], store_sem.at[2])

    @pl.when(is_root)
    def _():
        grad_v[...] = jnp.zeros_like(grad_v)

    @pl.when(jnp.logical_not(is_root))
    def _():
        factor[...] = -(factor_t[...].T)

        def act(d):
            for k in range(1, nx):
                near_copy(d, k).wait_recv()
        each_near(act)
        for d in range(2):
            which = d if d == 0 else jnp.where(is_last, 0, 1)
            full = jnp.concatenate([near[which, c] for c in range(nx)], axis=1)
            grad_v[d] = lax.dot_general(
                factor[...], full, (((1,), (1,)), ((), ())),
                preferred_element_type=F32).astype(BF16)

    low_store.start()
    up_store.start()

    for k in range(1, nx):
        src_copy(k).wait_recv()

    @pl.when(is_root)
    def _():
        total = src_t[...].astype(F32)
        for c in range(nx):
            pltpu.make_async_remote_copy(
                src_ref=root_out.at[c], dst_ref=root_in.at[c],
                send_sem=root_ss.at[c], recv_sem=root_rs.at[c],
                device_id=(row, other(1)), device_id_type=MESH).wait_recv()
        for c in range(nx):
            total = total - root_in[c].astype(F32)
        src_t[...] = total.astype(BF16)

    src_v[...] = src_t[...].T
    src_store.start()

    for k in range(1, nx):
        cot_copy(k).wait_send()
        src_copy(k).wait_send()
    each_sol(lambda c: c.wait_send())

    @pl.when(jnp.logical_not(is_root))
    def _():
        def act(d):
            for k in range(1, nx):
                near_copy(d, k).wait_send()
        each_near(act)

    @pl.when(level < last)
    def _():
        for k in range(nx):
            for d in range(2):
                push_copy(my_level, d, k, up_row(stride)).wait_send()

    @pl.when(is_last)
    def _():
        for k in range(nx):
            root_copy(k).wait_send()

    low_store.wait()
    up_store.wait()
    src_store.wait()


def body(n, nx, lower_coupling, upper_coupling, solution, cotangent):
    _, half, block = lower_coupling.shape
    width = cotangent.shape[2]
    full = width * nx
    levels = n.bit_length() - 1
    dma = pltpu.SemaphoreType.DMA
    return pl.pallas_call(
        functools.partial(kernel, n, nx),
        out_shape=(
            jax.ShapeDtypeStruct(cotangent.shape, BF16),
            jax.ShapeDtypeStruct(lower_coupling.shape, BF16),
            jax.ShapeDtypeStruct(upper_coupling.shape, BF16),
        ),
        in_specs=[pl.BlockSpec(memory_space=pl.ANY)] * 4,
        out_specs=[pl.BlockSpec(memory_space=pl.ANY)] * 3,
        scratch_shapes=[
            pltpu.VMEM((half, block), BF16),
            pltpu.VMEM((half, block), BF16),
            pltpu.VMEM((block, width), BF16),
            pltpu.VMEM((block, width), BF16),
            pltpu.VMEM((width, block), BF16),
            pltpu.VMEM((full, half), BF16),
            pltpu.VMEM((full, half), F32),
            pltpu.VMEM((full, half), BF16),
            pltpu.VMEM((half, full), BF16),
            pltpu.VMEM((2, nx, full, half), BF16),
            pltpu.VMEM((max(levels - 1, 1), 2, nx, full, half), BF16),
            pltpu.VMEM((nx, width, block), BF16),
            pltpu.VMEM((nx, width, block), BF16),
            pltpu.VMEM((2, nx, block, width), BF16),
            pltpu.VMEM((width, block), BF16),
            pltpu.VMEM((block, width), BF16),
            pltpu.VMEM((2, half, block), BF16),
            dma((4,)), dma((3,)),
            dma((nx,)), dma((nx,)),
            dma((2, nx)), dma((max(levels - 1, 1), 2, nx)),
            dma((nx,)), dma((nx,)),
            dma((levels, 2)), dma((2,)),
            dma((2, nx)), dma((2, nx)),
            dma((nx,)), dma((nx,)),
        ],
        compiler_params=pltpu.CompilerParams(
            collective_id=0, has_side_effects=True, vmem_limit_bytes=48 * 1024 * 1024),
    )(lower_coupling, upper_coupling, solution, cotangent)


def solution(mesh):
    in_specs = (
        P("rows", "cols", None),
        P("rows", "cols", None),
        P("rows", None, "cols"),
        P("rows", None, "cols"),
    )
    out_specs = (P("rows", None, "cols"), P("rows", "cols", None), P("rows", "cols", None))
    local = functools.partial(body, mesh.shape["rows"], mesh.shape["cols"])
    return jax.shard_map(local, mesh=mesh, in_specs=in_specs, out_specs=out_specs, check_vma=False)
```

```python
import functools

import jax
import jax.numpy as jnp
from jax import lax
from jax.experimental import pallas as pl
from jax.experimental.pallas import tpu as pltpu
from jax.sharding import PartitionSpec as P

MESH = pl.DeviceIdType.MESH
F32 = jnp.float32
BF16 = jnp.bfloat16


def kernel(n, nx, wide, lower_hbm, upper_hbm, sol_hbm, cot_hbm, src_out, low_out, up_out,
           mats, sol_v, cot_v, cot_t, cot_half, acc, factor_t, factor, half_out, half_in,
           acc_col, col_out, col_in, wide_out, wide_in, near, src_t, src_v, grad_v,
           load_sem, store_sem, cot_ss, cot_rs, half_ss, half_rs, col_ss, col_rs,
           wide_ss, wide_rs, gat_ss, gat_rs, sol_ss, sol_rs, near_ss, near_rs, src_ss, src_rs):
    block, width = cot_v.shape
    half = block // nx
    levels = n.bit_length() - 1
    last = levels - 1
    row = lax.axis_index("rows")
    col = lax.axis_index("cols")
    offset = lax.rem(row + n - 1, n)
    level = jnp.int32(0)
    for l in range(levels):
        level = level + jnp.where(lax.rem(offset, 2 << l) == 0, 1, 0)
    is_root = level == levels
    is_last = level == last
    is_half = level < wide
    is_col = (level >= wide) & (level < levels)
    stride = jnp.int32(1)
    for l in range(levels):
        stride = jnp.where(level > l, 2 << l, stride)
    stride = jnp.where(is_root, 0, stride)

    def other(k):
        return lax.rem(col + k, nx)

    def up_row(s):
        return lax.rem(row + s, n)

    def down_row(s):
        return lax.rem(row + n - s, n)

    loads = [
        pltpu.make_async_copy(cot_hbm.at[0], cot_v, load_sem.at[0]),
        pltpu.make_async_copy(lower_hbm.at[0], mats.at[1, col], load_sem.at[1]),
        pltpu.make_async_copy(upper_hbm.at[0], mats.at[0, col], load_sem.at[2]),
        pltpu.make_async_copy(sol_hbm.at[0], sol_v, load_sem.at[3]),
    ]
    for load in loads:
        load.start()

    barrier = pltpu.get_barrier_semaphore()
    for k in range(1, nx):
        pl.semaphore_signal(barrier, inc=1, device_id=(row, other(k)), device_id_type=MESH)
    for l in range(levels):
        @pl.when(level >= l)
        def _():
            for k in range(nx):
                pl.semaphore_signal(barrier, inc=1, device_id=(up_row(1 << l), k), device_id_type=MESH)
                if l != last:
                    pl.semaphore_signal(barrier, inc=1, device_id=(down_row(1 << l), k), device_id_type=MESH)

    loads[0].wait()
    cot_t[...] = cot_v[...].T
    low_half = pl.ds(pl.multiple_of(col * half, half), half)
    own_cols = pl.ds(pl.multiple_of(col * width, width), width)

    @pl.when(is_half)
    def _():
        cot_half[own_cols, :] = cot_t[:, low_half]

    reached = jnp.minimum(level + 1, last)
    pl.semaphore_wait(barrier, (nx - 1) + nx * (2 * reached + jnp.where(level >= last, 1, 0)))

    def cot_copy(k):
        to = other(k)
        return pltpu.make_async_remote_copy(
            src_ref=cot_t.at[:, pl.ds(pl.multiple_of(to * half, half), half)],
            dst_ref=cot_half.at[own_cols, :],
            send_sem=cot_ss.at[k], recv_sem=cot_rs.at[k],
            device_id=(row, to), device_id_type=MESH)

    def gather_copy(d, k):
        return pltpu.make_async_remote_copy(
            src_ref=(upper_hbm, lower_hbm)[d].at[0], dst_ref=mats.at[d, col],
            send_sem=gat_ss.at[d, k], recv_sem=gat_rs.at[d, k],
            device_id=(row, other(k)), device_id_type=MESH)

    @pl.when(is_half)
    def _():
        for k in range(1, nx):
            cot_copy(k).start()

    @pl.when(is_col)
    def _():
        for d in range(2):
            for k in range(1, nx):
                gather_copy(d, k).start()

    def sol_copy(l, d):
        target = up_row(1 << l) if d == 0 else down_row(1 << l)
        return pltpu.make_async_remote_copy(
            src_ref=sol_v, dst_ref=near.at[d, col],
            send_sem=sol_ss.at[l, d], recv_sem=sol_rs.at[d],
            device_id=(target, col), device_id_type=MESH)

    def each_sol(act):
        for l in range(levels):
            @pl.when(level > l)
            def _():
                for d in range(2 if l != last else 1):
                    act(sol_copy(l, d))


    def near_copy(d, k):
        return pltpu.make_async_remote_copy(
            src_ref=near.at[d, col], dst_ref=near.at[d, col],
            send_sem=near_ss.at[d, k], recv_sem=near_rs.at[d, k],
            device_id=(row, other(k)), device_id_type=MESH)

    def each_near(act):
        act(0)

        @pl.when(level < last)
        def _():
            act(1)

    def forward_near():
        def act(d):
            sol_copy(0, d).wait_recv()
            for k in range(1, nx):
                near_copy(d, k).start()
        each_near(act)

    def send_sol():
        each_sol(lambda c: c.start())

    def half_copy(k, l, d, target):
        to = other(k)
        return pltpu.make_async_remote_copy(
            src_ref=half_out.at[to], dst_ref=half_in.at[l, d, col],
            send_sem=half_ss.at[k], recv_sem=half_rs.at[l, d, col],
            device_id=(target, to), device_id_type=MESH)

    def col_copy(k, l, d, target):
        to = other(k)
        return pltpu.make_async_remote_copy(
            src_ref=col_out.at[d, to], dst_ref=col_in.at[l, d, col],
            send_sem=col_ss.at[d, k], recv_sem=col_rs.at[l, d, col],
            device_id=(target, to), device_id_type=MESH)

    def wide_copy(j, l, d, target):
        return pltpu.make_async_remote_copy(
            src_ref=wide_out.at[d, j], dst_ref=wide_in.at[l, d, j],
            send_sem=wide_ss.at[d, j], recv_sem=wide_rs.at[l, d, j],
            device_id=(target, col), device_id_type=MESH)

    def arrived(dst, sem):
        pltpu.make_async_remote_copy(
            src_ref=dst, dst_ref=dst, send_sem=sem, recv_sem=sem,
            device_id=(row, other(1)), device_id_type=MESH).wait_recv()

    def src_copy(k):
        to = other(k)
        return pltpu.make_async_remote_copy(
            src_ref=factor_t.at[pl.ds(pl.multiple_of(to * width, width), width), :],
            dst_ref=src_t.at[:, low_half],
            send_sem=src_ss.at[k], recv_sem=src_rs.at[k],
            device_id=(row, to), device_id_type=MESH)

    span = jnp.maximum(stride, 1)
    first = jnp.where(lax.rem(offset + span, 4 * span) == 2 * span, 0, 1)
    second = 1 - first

    def target_of(d):
        return jnp.where(d == 0, up_row(stride), down_row(stride))

    order = list(range(1, nx)) + [0]
    half_level = jnp.minimum(level, wide - 1)

    def fill_col(d):
        push = jnp.dot(factor_t[...], mats[d, col], preferred_element_type=F32).astype(BF16)
        for c in range(nx):
            col_out[d, c] = push[c * width:(c + 1) * width]

    @pl.when(is_half)
    def _():
        for k in range(1, nx):
            cot_copy(k).wait_recv()

        @pl.when(level == 0)
        def _():
            factor_t[...] = cot_half[...]

        for l in range(wide - 1):
            @pl.when(level > l)
            def _():
                if l == 0:
                    acc[...] = cot_half[...].astype(F32)
                total = None
                for c in range(nx):
                    for d in range(2):
                        arrived(half_in.at[l, d, c], half_rs.at[l, d, c])
                        term = half_in[l, d, c].astype(F32)
                        total = term if total is None else total + term
                acc[...] = acc[...] - total
                factor_t[...] = acc[...].astype(BF16)

        loads[1].wait()
        loads[2].wait()

        @pl.when(level < wide - 1)
        def _():
            for k in order:
                to = other(k)
                part = pl.ds(pl.multiple_of(to * half, half), half)
                half_out[to] = jnp.dot(
                    factor_t[...], mats[first, col, :, part], preferred_element_type=F32).astype(BF16)
                half_copy(k, jnp.minimum(half_level, max(wide - 2, 0)), first, target_of(first)).start()

        @pl.when(level == wide - 1)
        def _():
            fill_col(first)
            for k in order:
                col_copy(k, half_level, first, target_of(first)).start()

        fill_col(second)
        for k in order:
            col_copy(k, half_level, second, target_of(second)).start()
        for k in range(1, nx):
            src_copy(k).start()
        src_t[:, low_half] = factor_t[own_cols, :]
        loads[3].wait()
        send_sol()
        forward_near()

    @pl.when(level >= wide)
    def _():
        acc_col[...] = cot_t[...].astype(F32)
        for l in range(wide):
            total = None
            for c in range(nx):
                for d in range(2):
                    arrived(col_in.at[l, d, c], col_rs.at[l, d, c])
                    term = col_in[l, d, c].astype(F32)
                    total = term if total is None else total + term
            acc_col[...] = acc_col[...] - total
            if l == 0:
                loads[3].wait()
                send_sol()
        loads[1].wait()
        loads[2].wait()

        @pl.when((level > wide) & (level < levels))
        def _():
            forward_near()

        def add_wide(l, ds):
            for j in range(nx):
                total = None
                for d in ds:
                    arrived(wide_in.at[l, d, j], wide_rs.at[l, d, j])
                    term = wide_in[l, d, j].astype(F32)
                    total = term if total is None else total + term
                part = slice(j * half, (j + 1) * half)
                acc_col[:, part] = acc_col[:, part] - total

        for l in range(wide, last):
            @pl.when(level > l)
            def _():
                add_wide(l - wide, (0, 1))

        @pl.when(is_root)
        def _():
            add_wide(last - wide, (0,))
            src_t[...] = acc_col[...].astype(BF16)

    wide_level = jnp.maximum(jnp.minimum(level, last) - wide, 0)

    def product(d, j):
        total = None
        for c in range(nx):
            term = jnp.dot(cot_t[:, c * half:(c + 1) * half],
                           mats[d, c, :, j * half:(j + 1) * half], preferred_element_type=F32)
            total = term if total is None else total + term
        return total

    @pl.when(is_col)
    def _():
        cot_t[...] = acc_col[...].astype(BF16)
        src_t[...] = cot_t[...]
        for d in range(2):
            for k in range(1, nx):
                gather_copy(d, k).wait_recv()

        @pl.when(level < last)
        def _():
            for d in (first, second):
                for j in range(nx):
                    wide_out[d, j] = product(d, j).astype(BF16)
                    wide_copy(j, wide_level, d, target_of(d)).start()

        @pl.when(is_last)
        def _():
            for j in range(nx):
                wide_out[0, j] = (product(0, j) + product(1, j)).astype(BF16)
                wide_copy(j, wide_level, 0, up_row(1 << last)).start()

        for k in range(1, nx):
            cot_copy(k).start()
        cot_half[own_cols, :] = cot_t[:, low_half]

        @pl.when(level == wide)
        def _():
            forward_near()

        for k in range(1, nx):
            cot_copy(k).wait_recv()
        factor_t[...] = cot_half[...]

    low_store = pltpu.make_async_copy(grad_v.at[0], low_out.at[0], store_sem.at[0])
    up_store = pltpu.make_async_copy(grad_v.at[1], up_out.at[0], store_sem.at[1])
    src_store = pltpu.make_async_copy(src_v, src_out.at[0], store_sem.at[2])

    @pl.when(is_root)
    def _():
        grad_v[...] = jnp.zeros_like(grad_v)

    @pl.when(jnp.logical_not(is_root))
    def _():
        factor[...] = -(factor_t[...].T)

        def act(d):
            for k in range(1, nx):
                near_copy(d, k).wait_recv()
        each_near(act)
        for d in range(2):
            which = d if d == 0 else jnp.where(is_last, 0, 1)
            full = jnp.concatenate([near[which, c] for c in range(nx)], axis=1)
            grad_v[d] = lax.dot_general(
                factor[...], full, (((1,), (1,)), ((), ())),
                preferred_element_type=F32).astype(BF16)

    low_store.start()
    up_store.start()

    @pl.when(is_half)
    def _():
        for k in range(1, nx):
            src_copy(k).wait_recv()

    src_v[...] = src_t[...].T
    src_store.start()

    each_sol(lambda c: c.wait_send())

    @pl.when(jnp.logical_not(is_root))
    def _():
        def act(d):
            for k in range(1, nx):
                near_copy(d, k).wait_send()
        each_near(act)
        for k in range(1, nx):
            cot_copy(k).wait_send()

    @pl.when(is_half)
    def _():
        for k in range(1, nx):
            src_copy(k).wait_send()
        for k in range(nx):
            col_copy(k, half_level, second, row).wait_send()

        @pl.when(level < wide - 1)
        def _():
            for k in range(nx):
                half_copy(k, 0, first, row).wait_send()

        @pl.when(level == wide - 1)
        def _():
            for k in range(nx):
                col_copy(k, half_level, first, row).wait_send()

    @pl.when(is_col)
    def _():
        for d in range(2):
            for k in range(1, nx):
                gather_copy(d, k).wait_send()
        for j in range(nx):
            wide_copy(j, wide_level, 0, row).wait_send()

            @pl.when(level < last)
            def _():
                wide_copy(j, wide_level, 1, row).wait_send()

    low_store.wait()
    up_store.wait()
    src_store.wait()


def body(n, nx, lower_coupling, upper_coupling, solution, cotangent):
    _, half, block = lower_coupling.shape
    width = cotangent.shape[2]
    full = width * nx
    levels = n.bit_length() - 1
    wide = min(2, levels - 1)
    dma = pltpu.SemaphoreType.DMA
    return pl.pallas_call(
        functools.partial(kernel, n, nx, wide),
        out_shape=(
            jax.ShapeDtypeStruct(cotangent.shape, BF16),
            jax.ShapeDtypeStruct(lower_coupling.shape, BF16),
            jax.ShapeDtypeStruct(upper_coupling.shape, BF16),
        ),
        in_specs=[pl.BlockSpec(memory_space=pl.ANY)] * 4,
        out_specs=[pl.BlockSpec(memory_space=pl.ANY)] * 3,
        scratch_shapes=[
            pltpu.VMEM((2, nx, half, block), BF16),
            pltpu.VMEM((block, width), BF16),
            pltpu.VMEM((block, width), BF16),
            pltpu.VMEM((width, block), BF16),
            pltpu.VMEM((full, half), BF16),
            pltpu.VMEM((full, half), F32),
            pltpu.VMEM((full, half), BF16),
            pltpu.VMEM((half, full), BF16),
            pltpu.VMEM((nx, full, half), BF16),
            pltpu.VMEM((max(wide - 1, 1), 2, nx, full, half), BF16),
            pltpu.VMEM((width, block), F32),
            pltpu.VMEM((2, nx, width, block), BF16),
            pltpu.VMEM((wide, 2, nx, width, block), BF16),
            pltpu.VMEM((2, nx, width, half), BF16),
            pltpu.VMEM((levels - wide, 2, nx, width, half), BF16),
            pltpu.VMEM((2, nx, block, width), BF16),
            pltpu.VMEM((width, block), BF16),
            pltpu.VMEM((block, width), BF16),
            pltpu.VMEM((2, half, block), BF16),
            dma((4,)), dma((3,)),
            dma((nx,)), dma((nx,)),
            dma((nx,)), dma((max(wide - 1, 1), 2, nx)),
            dma((2, nx)), dma((wide, 2, nx)),
            dma((2, nx)), dma((levels - wide, 2, nx)),
            dma((2, nx)), dma((2, nx)),
            dma((levels, 2)), dma((2,)),
            dma((2, nx)), dma((2, nx)),
            dma((nx,)), dma((nx,)),
        ],
        compiler_params=pltpu.CompilerParams(
            collective_id=0, has_side_effects=True, vmem_limit_bytes=62 * 1024 * 1024),
    )(lower_coupling, upper_coupling, solution, cotangent)


def solution(mesh):
    in_specs = (
        P("rows", "cols", None),
        P("rows", "cols", None),
        P("rows", None, "cols"),
        P("rows", None, "cols"),
    )
    out_specs = (P("rows", None, "cols"), P("rows", "cols", None), P("rows", "cols", None))
    local = functools.partial(body, mesh.shape["rows"], mesh.shape["cols"])
    return jax.shard_map(local, mesh=mesh, in_specs=in_specs, out_specs=out_specs, check_vma=False)
```

```python
import functools

import jax
import jax.numpy as jnp
from jax import lax
from jax.experimental import pallas as pl
from jax.experimental.pallas import tpu as pltpu
from jax.sharding import PartitionSpec as P

MESH = pl.DeviceIdType.MESH
F32 = jnp.float32
BF16 = jnp.bfloat16


def kernel(n, nx, wide, lower_hbm, upper_hbm, sol_hbm, cot_hbm, src_out, low_out, up_out,
           mats, sol_v, cot_v, cot_t, cot_half, acc, factor_t, factor, half_out, half_in,
           acc_col, col_out, col_in, wide_out, wide_in, near, src_t, src_v, grad_v,
           load_sem, store_sem, cot_ss, cot_rs, half_ss, half_rs, col_ss, col_rs,
           wide_ss, wide_rs, gat_ss, gat_rs, sol_ss, sol_rs, near_ss, near_rs, src_ss, src_rs):
    block, width = cot_v.shape
    half = block // nx
    levels = n.bit_length() - 1
    last = levels - 1
    row = lax.axis_index("rows")
    col = lax.axis_index("cols")
    offset = lax.rem(row + n - 1, n)
    level = jnp.int32(0)
    for l in range(levels):
        level = level + jnp.where(lax.rem(offset, 2 << l) == 0, 1, 0)
    is_root = level == levels
    is_last = level == last
    is_half = level < wide
    is_col = (level >= wide) & (level < levels)
    stride = jnp.int32(1)
    for l in range(levels):
        stride = jnp.where(level > l, 2 << l, stride)
    stride = jnp.where(is_root, 0, stride)

    span = jnp.maximum(stride, 1)
    first = jnp.where(lax.rem(offset + span, 4 * span) == 2 * span, 0, 1)
    second = 1 - first

    def other(k):
        return lax.rem(col + k, nx)

    def up_row(s):
        return lax.rem(row + s, n)

    def down_row(s):
        return lax.rem(row + n - s, n)

    loads = [
        pltpu.make_async_copy(cot_hbm.at[0], cot_v, load_sem.at[0]),
        pltpu.make_async_copy(lower_hbm.at[0], mats.at[1, col], load_sem.at[1]),
        pltpu.make_async_copy(upper_hbm.at[0], mats.at[0, col], load_sem.at[2]),
        pltpu.make_async_copy(sol_hbm.at[0], sol_v, load_sem.at[3]),
    ]
    for load in loads:
        load.start()

    barrier = pltpu.get_barrier_semaphore()
    for k in range(1, nx):
        pl.semaphore_signal(barrier, inc=1, device_id=(row, other(k)), device_id_type=MESH)
    for l in range(levels):
        @pl.when(level >= l)
        def _():
            for k in range(nx):
                pl.semaphore_signal(barrier, inc=1, device_id=(up_row(1 << l), k), device_id_type=MESH)
                if l != last:
                    pl.semaphore_signal(barrier, inc=1, device_id=(down_row(1 << l), k), device_id_type=MESH)

    loads[0].wait()
    cot_t[...] = cot_v[...].T
    low_half = pl.ds(pl.multiple_of(col * half, half), half)
    own_cols = pl.ds(pl.multiple_of(col * width, width), width)

    @pl.when(is_half)
    def _():
        cot_half[own_cols, :] = cot_t[:, low_half]

    reached = jnp.minimum(level + 1, last)
    pl.semaphore_wait(barrier, (nx - 1) + nx * (2 * reached + jnp.where(level >= last, 1, 0)))

    def cot_copy(k):
        to = other(k)
        return pltpu.make_async_remote_copy(
            src_ref=cot_t.at[:, pl.ds(pl.multiple_of(to * half, half), half)],
            dst_ref=cot_half.at[own_cols, :],
            send_sem=cot_ss.at[k], recv_sem=cot_rs.at[k],
            device_id=(row, to), device_id_type=MESH)

    def gather_copy(d, k):
        return pltpu.make_async_remote_copy(
            src_ref=(upper_hbm, lower_hbm)[d].at[0], dst_ref=mats.at[d, col],
            send_sem=gat_ss.at[d, k], recv_sem=gat_rs.at[d, k],
            device_id=(row, other(k)), device_id_type=MESH)

    def gather(which, act):
        for d in range(2):
            @pl.when(which == d)
            def _():
                for k in range(1, nx):
                    act(gather_copy(d, k))

    @pl.when(is_half)
    def _():
        for k in range(1, nx):
            cot_copy(k).start()

    @pl.when(is_col)
    def _():
        gather(first, lambda c: c.start())

    def sol_copy(l, d):
        target = up_row(1 << l) if d == 0 else down_row(1 << l)
        return pltpu.make_async_remote_copy(
            src_ref=sol_v, dst_ref=near.at[d, col],
            send_sem=sol_ss.at[l, d], recv_sem=sol_rs.at[d],
            device_id=(target, col), device_id_type=MESH)

    def each_sol(act):
        for l in range(levels):
            @pl.when(level > l)
            def _():
                for d in range(2 if l != last else 1):
                    act(sol_copy(l, d))


    def near_copy(d, k):
        return pltpu.make_async_remote_copy(
            src_ref=near.at[d, col], dst_ref=near.at[d, col],
            send_sem=near_ss.at[d, k], recv_sem=near_rs.at[d, k],
            device_id=(row, other(k)), device_id_type=MESH)

    def each_near(act):
        act(0)

        @pl.when(level < last)
        def _():
            act(1)

    def forward_near():
        def act(d):
            sol_copy(0, d).wait_recv()
            for k in range(1, nx):
                near_copy(d, k).start()
        each_near(act)

    def send_sol():
        each_sol(lambda c: c.start())

    def half_copy(k, l, d, target):
        to = other(k)
        return pltpu.make_async_remote_copy(
            src_ref=half_out.at[to], dst_ref=half_in.at[l, d, col],
            send_sem=half_ss.at[k], recv_sem=half_rs.at[l, d, col],
            device_id=(target, to), device_id_type=MESH)

    def col_copy(k, l, d, target):
        to = other(k)
        return pltpu.make_async_remote_copy(
            src_ref=col_out.at[d, to], dst_ref=col_in.at[l, d, col],
            send_sem=col_ss.at[d, k], recv_sem=col_rs.at[l, d, col],
            device_id=(target, to), device_id_type=MESH)

    def wide_copy(j, l, d, target):
        return pltpu.make_async_remote_copy(
            src_ref=wide_out.at[d, j], dst_ref=wide_in.at[l, d, j],
            send_sem=wide_ss.at[d, j], recv_sem=wide_rs.at[l, d, j],
            device_id=(target, col), device_id_type=MESH)

    def arrived(dst, sem):
        pltpu.make_async_remote_copy(
            src_ref=dst, dst_ref=dst, send_sem=sem, recv_sem=sem,
            device_id=(row, other(1)), device_id_type=MESH).wait_recv()

    def src_copy(k):
        to = other(k)
        return pltpu.make_async_remote_copy(
            src_ref=factor_t.at[pl.ds(pl.multiple_of(to * width, width), width), :],
            dst_ref=src_t.at[:, low_half],
            send_sem=src_ss.at[k], recv_sem=src_rs.at[k],
            device_id=(row, to), device_id_type=MESH)


    def target_of(d):
        return jnp.where(d == 0, up_row(stride), down_row(stride))

    order = list(range(1, nx)) + [0]
    half_level = jnp.minimum(level, wide - 1)

    def fill_col(d):
        push = jnp.dot(factor_t[...], mats[d, col], preferred_element_type=F32).astype(BF16)
        for c in range(nx):
            col_out[d, c] = push[c * width:(c + 1) * width]

    @pl.when(is_half)
    def _():
        for k in range(1, nx):
            cot_copy(k).wait_recv()

        @pl.when(level == 0)
        def _():
            factor_t[...] = cot_half[...]

        for l in range(wide - 1):
            @pl.when(level > l)
            def _():
                if l == 0:
                    acc[...] = cot_half[...].astype(F32)
                total = None
                for c in range(nx):
                    for d in range(2):
                        arrived(half_in.at[l, d, c], half_rs.at[l, d, c])
                        term = half_in[l, d, c].astype(F32)
                        total = term if total is None else total + term
                acc[...] = acc[...] - total
                factor_t[...] = acc[...].astype(BF16)

        loads[1].wait()
        loads[2].wait()

        @pl.when(level < wide - 1)
        def _():
            for k in order:
                to = other(k)
                part = pl.ds(pl.multiple_of(to * half, half), half)
                half_out[to] = jnp.dot(
                    factor_t[...], mats[first, col, :, part], preferred_element_type=F32).astype(BF16)
                half_copy(k, jnp.minimum(half_level, max(wide - 2, 0)), first, target_of(first)).start()

        @pl.when(level == wide - 1)
        def _():
            fill_col(first)
            for k in order:
                col_copy(k, half_level, first, target_of(first)).start()

        fill_col(second)
        for k in order:
            col_copy(k, half_level, second, target_of(second)).start()
        for k in range(1, nx):
            src_copy(k).start()
        src_t[:, low_half] = factor_t[own_cols, :]
        loads[3].wait()
        send_sol()
        forward_near()

    @pl.when(level >= wide)
    def _():
        acc_col[...] = cot_t[...].astype(F32)
        for l in range(wide):
            total = None
            for c in range(nx):
                for d in range(2):
                    arrived(col_in.at[l, d, c], col_rs.at[l, d, c])
                    term = col_in[l, d, c].astype(F32)
                    total = term if total is None else total + term
            acc_col[...] = acc_col[...] - total
            if l == 0:
                @pl.when(is_col)
                def _():
                    gather(second, lambda c: c.start())

                loads[3].wait()
                send_sol()
        loads[1].wait()
        loads[2].wait()

        @pl.when((level > wide) & (level < levels))
        def _():
            forward_near()

        def add_wide(l, ds):
            for j in range(nx):
                total = None
                for d in ds:
                    arrived(wide_in.at[l, d, j], wide_rs.at[l, d, j])
                    term = wide_in[l, d, j].astype(F32)
                    total = term if total is None else total + term
                part = slice(j * half, (j + 1) * half)
                acc_col[:, part] = acc_col[:, part] - total

        for l in range(wide, last):
            @pl.when(level > l)
            def _():
                add_wide(l - wide, (0, 1))

        @pl.when(is_root)
        def _():
            add_wide(last - wide, (0,))
            src_t[...] = acc_col[...].astype(BF16)

    wide_level = jnp.maximum(jnp.minimum(level, last) - wide, 0)

    def product(d, j):
        total = None
        for c in range(nx):
            term = jnp.dot(cot_t[:, c * half:(c + 1) * half],
                           mats[d, c, :, j * half:(j + 1) * half], preferred_element_type=F32)
            total = term if total is None else total + term
        return total

    @pl.when(is_col)
    def _():
        cot_t[...] = acc_col[...].astype(BF16)
        src_t[...] = cot_t[...]
        gather(first, lambda c: c.wait_recv())

        @pl.when(level < last)
        def _():
            for d in (first, second):
                if d is second:
                    gather(second, lambda c: c.wait_recv())
                for j in range(nx):
                    wide_out[d, j] = product(d, j).astype(BF16)
                    wide_copy(j, wide_level, d, target_of(d)).start()

        @pl.when(is_last)
        def _():
            gather(second, lambda c: c.wait_recv())
            for j in range(nx):
                wide_out[0, j] = (product(0, j) + product(1, j)).astype(BF16)
                wide_copy(j, wide_level, 0, up_row(1 << last)).start()

        for k in range(1, nx):
            cot_copy(k).start()
        cot_half[own_cols, :] = cot_t[:, low_half]

        @pl.when(level == wide)
        def _():
            forward_near()

        for k in range(1, nx):
            cot_copy(k).wait_recv()
        factor_t[...] = cot_half[...]

    low_store = pltpu.make_async_copy(grad_v.at[0], low_out.at[0], store_sem.at[0])
    up_store = pltpu.make_async_copy(grad_v.at[1], up_out.at[0], store_sem.at[1])
    src_store = pltpu.make_async_copy(src_v, src_out.at[0], store_sem.at[2])

    @pl.when(is_root)
    def _():
        grad_v[...] = jnp.zeros_like(grad_v)

    @pl.when(jnp.logical_not(is_root))
    def _():
        factor[...] = -(factor_t[...].T)

        def act(d):
            for k in range(1, nx):
                near_copy(d, k).wait_recv()
        each_near(act)
        for d in range(2):
            which = d if d == 0 else jnp.where(is_last, 0, 1)
            full = jnp.concatenate([near[which, c] for c in range(nx)], axis=1)
            grad_v[d] = lax.dot_general(
                factor[...], full, (((1,), (1,)), ((), ())),
                preferred_element_type=F32).astype(BF16)

    low_store.start()
    up_store.start()

    @pl.when(is_half)
    def _():
        for k in range(1, nx):
            src_copy(k).wait_recv()

    src_v[...] = src_t[...].T
    src_store.start()

    each_sol(lambda c: c.wait_send())

    @pl.when(jnp.logical_not(is_root))
    def _():
        def act(d):
            for k in range(1, nx):
                near_copy(d, k).wait_send()
        each_near(act)
        for k in range(1, nx):
            cot_copy(k).wait_send()

    @pl.when(is_half)
    def _():
        for k in range(1, nx):
            src_copy(k).wait_send()
        for k in range(nx):
            col_copy(k, half_level, second, row).wait_send()

        @pl.when(level < wide - 1)
        def _():
            for k in range(nx):
                half_copy(k, 0, first, row).wait_send()

        @pl.when(level == wide - 1)
        def _():
            for k in range(nx):
                col_copy(k, half_level, first, row).wait_send()

    @pl.when(is_col)
    def _():
        for d in range(2):
            for k in range(1, nx):
                gather_copy(d, k).wait_send()
        for j in range(nx):
            wide_copy(j, wide_level, 0, row).wait_send()

            @pl.when(level < last)
            def _():
                wide_copy(j, wide_level, 1, row).wait_send()

    low_store.wait()
    up_store.wait()
    src_store.wait()


def body(n, nx, lower_coupling, upper_coupling, solution, cotangent):
    _, half, block = lower_coupling.shape
    width = cotangent.shape[2]
    full = width * nx
    levels = n.bit_length() - 1
    wide = min(2, levels - 1)
    dma = pltpu.SemaphoreType.DMA
    return pl.pallas_call(
        functools.partial(kernel, n, nx, wide),
        out_shape=(
            jax.ShapeDtypeStruct(cotangent.shape, BF16),
            jax.ShapeDtypeStruct(lower_coupling.shape, BF16),
            jax.ShapeDtypeStruct(upper_coupling.shape, BF16),
        ),
        in_specs=[pl.BlockSpec(memory_space=pl.ANY)] * 4,
        out_specs=[pl.BlockSpec(memory_space=pl.ANY)] * 3,
        scratch_shapes=[
            pltpu.VMEM((2, nx, half, block), BF16),
            pltpu.VMEM((block, width), BF16),
            pltpu.VMEM((block, width), BF16),
            pltpu.VMEM((width, block), BF16),
            pltpu.VMEM((full, half), BF16),
            pltpu.VMEM((full, half), F32),
            pltpu.VMEM((full, half), BF16),
            pltpu.VMEM((half, full), BF16),
            pltpu.VMEM((nx, full, half), BF16),
            pltpu.VMEM((max(wide - 1, 1), 2, nx, full, half), BF16),
            pltpu.VMEM((width, block), F32),
            pltpu.VMEM((2, nx, width, block), BF16),
            pltpu.VMEM((wide, 2, nx, width, block), BF16),
            pltpu.VMEM((2, nx, width, half), BF16),
            pltpu.VMEM((levels - wide, 2, nx, width, half), BF16),
            pltpu.VMEM((2, nx, block, width), BF16),
            pltpu.VMEM((width, block), BF16),
            pltpu.VMEM((block, width), BF16),
            pltpu.VMEM((2, half, block), BF16),
            dma((4,)), dma((3,)),
            dma((nx,)), dma((nx,)),
            dma((nx,)), dma((max(wide - 1, 1), 2, nx)),
            dma((2, nx)), dma((wide, 2, nx)),
            dma((2, nx)), dma((levels - wide, 2, nx)),
            dma((2, nx)), dma((2, nx)),
            dma((levels, 2)), dma((2,)),
            dma((2, nx)), dma((2, nx)),
            dma((nx,)), dma((nx,)),
        ],
        compiler_params=pltpu.CompilerParams(
            collective_id=0, has_side_effects=True, vmem_limit_bytes=62 * 1024 * 1024),
    )(lower_coupling, upper_coupling, solution, cotangent)


def solution(mesh):
    in_specs = (
        P("rows", "cols", None),
        P("rows", "cols", None),
        P("rows", None, "cols"),
        P("rows", None, "cols"),
    )
    out_specs = (P("rows", None, "cols"), P("rows", "cols", None), P("rows", "cols", None))
    local = functools.partial(body, mesh.shape["rows"], mesh.shape["cols"])
    return jax.shard_map(local, mesh=mesh, in_specs=in_specs, out_specs=out_specs, check_vma=False)
```

```python
import functools

import jax
import jax.numpy as jnp
from jax import lax
from jax.experimental import pallas as pl
from jax.experimental.pallas import tpu as pltpu
from jax.sharding import PartitionSpec as P

MESH = pl.DeviceIdType.MESH
F32 = jnp.float32
BF16 = jnp.bfloat16


def kernel(n, nx, wide, lower_hbm, upper_hbm, sol_hbm, cot_hbm, src_out, low_out, up_out,
           mats, sol_v, cot_v, cot_t, cot_half, acc, factor_t, factor, half_out, half_in,
           acc_col, col_out, col_in, wide_out, wide_in, near, src_t, src_v, grad_v,
           load_sem, store_sem, cot_ss, cot_rs, half_ss, half_rs, col_ss, col_rs,
           wide_ss, wide_rs, gat_ss, gat_rs, sol_ss, sol_rs, near_ss, near_rs, src_ss, src_rs):
    block, width = cot_v.shape
    half = block // nx
    levels = n.bit_length() - 1
    last = levels - 1
    row = lax.axis_index("rows")
    col = lax.axis_index("cols")
    offset = lax.rem(row + n - 1, n)
    level = jnp.int32(0)
    for l in range(levels):
        level = level + jnp.where(lax.rem(offset, 2 << l) == 0, 1, 0)
    is_root = level == levels
    is_last = level == last
    is_half = level < wide
    is_col = (level >= wide) & (level < levels)
    stride = jnp.int32(1)
    for l in range(levels):
        stride = jnp.where(level > l, 2 << l, stride)
    stride = jnp.where(is_root, 0, stride)

    span = jnp.maximum(stride, 1)
    first = jnp.where(lax.rem(offset + span, 4 * span) == 2 * span, 0, 1)
    second = 1 - first

    def other(k):
        return lax.rem(col + k, nx)

    def up_row(s):
        return lax.rem(row + s, n)

    def down_row(s):
        return lax.rem(row + n - s, n)

    loads = [
        pltpu.make_async_copy(cot_hbm.at[0], cot_v, load_sem.at[0]),
        pltpu.make_async_copy(lower_hbm.at[0], mats.at[1, col], load_sem.at[1]),
        pltpu.make_async_copy(upper_hbm.at[0], mats.at[0, col], load_sem.at[2]),
        pltpu.make_async_copy(sol_hbm.at[0], sol_v, load_sem.at[3]),
    ]
    for load in loads:
        load.start()

    barrier = pltpu.get_barrier_semaphore()
    for k in range(1, nx):
        pl.semaphore_signal(barrier, inc=1, device_id=(row, other(k)), device_id_type=MESH)
    for l in range(levels):
        @pl.when(level >= l)
        def _():
            for k in range(nx):
                pl.semaphore_signal(barrier, inc=1, device_id=(up_row(1 << l), k), device_id_type=MESH)
                if l != last:
                    pl.semaphore_signal(barrier, inc=1, device_id=(down_row(1 << l), k), device_id_type=MESH)

    loads[0].wait()
    cot_t[...] = cot_v[...].T
    low_half = pl.ds(pl.multiple_of(col * half, half), half)
    own_cols = pl.ds(pl.multiple_of(col * width, width), width)

    @pl.when(is_half)
    def _():
        cot_half[own_cols, :] = cot_t[:, low_half]

    reached = jnp.minimum(level + 1, last)
    pl.semaphore_wait(barrier, (nx - 1) + nx * (2 * reached + jnp.where(level >= last, 1, 0)))

    def cot_copy(k):
        to = other(k)
        return pltpu.make_async_remote_copy(
            src_ref=cot_t.at[:, pl.ds(pl.multiple_of(to * half, half), half)],
            dst_ref=cot_half.at[own_cols, :],
            send_sem=cot_ss.at[k], recv_sem=cot_rs.at[k],
            device_id=(row, to), device_id_type=MESH)

    def gather_copy(d, k):
        return pltpu.make_async_remote_copy(
            src_ref=(upper_hbm, lower_hbm)[d].at[0], dst_ref=mats.at[d, col],
            send_sem=gat_ss.at[d, k], recv_sem=gat_rs.at[d, k],
            device_id=(row, other(k)), device_id_type=MESH)

    def gather(which, act):
        for d in range(2):
            @pl.when(which == d)
            def _():
                for k in range(1, nx):
                    act(gather_copy(d, k))

    @pl.when(is_half)
    def _():
        for k in range(1, nx):
            cot_copy(k).start()

    @pl.when(is_col)
    def _():
        gather(first, lambda c: c.start())

    def sol_copy(l, d):
        target = up_row(1 << l) if d == 0 else down_row(1 << l)
        return pltpu.make_async_remote_copy(
            src_ref=sol_v, dst_ref=near.at[d, col],
            send_sem=sol_ss.at[l, d], recv_sem=sol_rs.at[d],
            device_id=(target, col), device_id_type=MESH)

    def each_sol(act):
        for l in range(levels):
            @pl.when(level > l)
            def _():
                for d in range(2 if l != last else 1):
                    act(sol_copy(l, d))


    def near_copy(d, k):
        return pltpu.make_async_remote_copy(
            src_ref=near.at[d, col], dst_ref=near.at[d, col],
            send_sem=near_ss.at[d, k], recv_sem=near_rs.at[d, k],
            device_id=(row, other(k)), device_id_type=MESH)

    def each_near(act):
        act(0)

        @pl.when(level < last)
        def _():
            act(1)

    def forward_near():
        def act(d):
            sol_copy(0, d).wait_recv()
            for k in range(1, nx):
                near_copy(d, k).start()
        each_near(act)

    def send_sol():
        each_sol(lambda c: c.start())

    def half_copy(k, l, d, target):
        to = other(k)
        return pltpu.make_async_remote_copy(
            src_ref=half_out.at[to], dst_ref=half_in.at[l, d, col],
            send_sem=half_ss.at[k], recv_sem=half_rs.at[l, d, col],
            device_id=(target, to), device_id_type=MESH)

    def col_copy(k, l, d, target):
        to = other(k)
        return pltpu.make_async_remote_copy(
            src_ref=col_out.at[d, to], dst_ref=col_in.at[l, d, col],
            send_sem=col_ss.at[d, k], recv_sem=col_rs.at[l, d, col],
            device_id=(target, to), device_id_type=MESH)

    def wide_copy(j, l, d, target):
        return pltpu.make_async_remote_copy(
            src_ref=wide_out.at[d, j], dst_ref=wide_in.at[l, d, j],
            send_sem=wide_ss.at[d, j], recv_sem=wide_rs.at[l, d, j],
            device_id=(target, col), device_id_type=MESH)

    def arrived(dst, sem):
        pltpu.make_async_remote_copy(
            src_ref=dst, dst_ref=dst, send_sem=sem, recv_sem=sem,
            device_id=(row, other(1)), device_id_type=MESH).wait_recv()

    def src_copy(k):
        to = other(k)
        return pltpu.make_async_remote_copy(
            src_ref=factor_t.at[pl.ds(pl.multiple_of(to * width, width), width), :],
            dst_ref=src_t.at[:, low_half],
            send_sem=src_ss.at[k], recv_sem=src_rs.at[k],
            device_id=(row, to), device_id_type=MESH)


    def target_of(d):
        return jnp.where(d == 0, up_row(stride), down_row(stride))

    order = list(range(1, nx)) + [0]
    half_level = jnp.minimum(level, wide - 1)

    def fill_col(d):
        push = jnp.dot(factor_t[...], mats[d, col], preferred_element_type=F32).astype(BF16)
        for c in range(nx):
            col_out[d, c] = push[c * width:(c + 1) * width]

    @pl.when(is_half)
    def _():
        for k in range(1, nx):
            cot_copy(k).wait_recv()

        @pl.when(level == 0)
        def _():
            factor_t[...] = cot_half[...]

        for l in range(wide - 1):
            @pl.when(level > l)
            def _():
                if l == 0:
                    acc[...] = cot_half[...].astype(F32)
                total = None
                for c in range(nx):
                    for d in range(2):
                        arrived(half_in.at[l, d, c], half_rs.at[l, d, c])
                        term = half_in[l, d, c].astype(F32)
                        total = term if total is None else total + term
                acc[...] = acc[...] - total
                factor_t[...] = acc[...].astype(BF16)

        loads[1].wait()
        loads[2].wait()

        @pl.when(level < wide - 1)
        def _():
            for k in order:
                to = other(k)
                part = pl.ds(pl.multiple_of(to * half, half), half)
                half_out[to] = jnp.dot(
                    factor_t[...], mats[first, col, :, part], preferred_element_type=F32).astype(BF16)
                half_copy(k, jnp.minimum(half_level, max(wide - 2, 0)), first, target_of(first)).start()

        @pl.when(level == wide - 1)
        def _():
            fill_col(first)
            for k in order:
                col_copy(k, half_level, first, target_of(first)).start()

        fill_col(second)
        for k in order:
            col_copy(k, half_level, second, target_of(second)).start()
        for k in range(1, nx):
            src_copy(k).start()
        src_t[:, low_half] = factor_t[own_cols, :]
        loads[3].wait()
        send_sol()
        forward_near()

    low_store = pltpu.make_async_copy(grad_v.at[0], low_out.at[0], store_sem.at[0])
    up_store = pltpu.make_async_copy(grad_v.at[1], up_out.at[0], store_sem.at[1])

    @pl.when(is_root)
    def _():
        grad_v[...] = jnp.zeros_like(grad_v)
        low_store.start()
        up_store.start()

    @pl.when(level >= wide)
    def _():
        acc_col[...] = cot_t[...].astype(F32)
        for l in range(wide):
            total = None
            for c in range(nx):
                for d in range(2):
                    arrived(col_in.at[l, d, c], col_rs.at[l, d, c])
                    term = col_in[l, d, c].astype(F32)
                    total = term if total is None else total + term
            acc_col[...] = acc_col[...] - total
            if l == 0:
                @pl.when(is_col)
                def _():
                    gather(second, lambda c: c.start())

                loads[3].wait()
                send_sol()
        loads[1].wait()
        loads[2].wait()

        @pl.when((level > wide) & (level < levels))
        def _():
            forward_near()

        def add_wide(l, ds):
            for j in range(nx):
                total = None
                for d in ds:
                    arrived(wide_in.at[l, d, j], wide_rs.at[l, d, j])
                    term = wide_in[l, d, j].astype(F32)
                    total = term if total is None else total + term
                part = slice(j * half, (j + 1) * half)
                acc_col[:, part] = acc_col[:, part] - total

        for l in range(wide, last):
            @pl.when(level > l)
            def _():
                add_wide(l - wide, (0, 1))

        @pl.when(is_root)
        def _():
            add_wide(last - wide, (0,))
            src_t[...] = acc_col[...].astype(BF16)

    wide_level = jnp.maximum(jnp.minimum(level, last) - wide, 0)

    def product(d, j):
        total = None
        for c in range(nx):
            term = jnp.dot(cot_t[:, c * half:(c + 1) * half],
                           mats[d, c, :, j * half:(j + 1) * half], preferred_element_type=F32)
            total = term if total is None else total + term
        return total

    @pl.when(is_col)
    def _():
        cot_t[...] = acc_col[...].astype(BF16)
        src_t[...] = cot_t[...]
        gather(first, lambda c: c.wait_recv())

        @pl.when(level < last)
        def _():
            for d in (first, second):
                if d is second:
                    gather(second, lambda c: c.wait_recv())
                for j in range(nx):
                    wide_out[d, j] = product(d, j).astype(BF16)
                    wide_copy(j, wide_level, d, target_of(d)).start()

        @pl.when(is_last)
        def _():
            gather(second, lambda c: c.wait_recv())
            for j in range(nx):
                wide_out[0, j] = (product(0, j) + product(1, j)).astype(BF16)
                wide_copy(j, wide_level, 0, up_row(1 << last)).start()

        for k in range(1, nx):
            cot_copy(k).start()
        cot_half[own_cols, :] = cot_t[:, low_half]

        @pl.when(level == wide)
        def _():
            forward_near()

        for k in range(1, nx):
            cot_copy(k).wait_recv()
        factor_t[...] = cot_half[...]

    src_store = pltpu.make_async_copy(src_v, src_out.at[0], store_sem.at[2])

    @pl.when(jnp.logical_not(is_root))
    def _():
        factor[...] = -(factor_t[...].T)

        def act(d):
            for k in range(1, nx):
                near_copy(d, k).wait_recv()
        each_near(act)
        for d in range(2):
            which = d if d == 0 else jnp.where(is_last, 0, 1)
            full = jnp.concatenate([near[which, c] for c in range(nx)], axis=1)
            grad_v[d] = lax.dot_general(
                factor[...], full, (((1,), (1,)), ((), ())),
                preferred_element_type=F32).astype(BF16)

        low_store.start()
        up_store.start()

    @pl.when(is_half)
    def _():
        for k in range(1, nx):
            src_copy(k).wait_recv()

    src_v[...] = src_t[...].T
    src_store.start()

    each_sol(lambda c: c.wait_send())

    @pl.when(jnp.logical_not(is_root))
    def _():
        def act(d):
            for k in range(1, nx):
                near_copy(d, k).wait_send()
        each_near(act)
        for k in range(1, nx):
            cot_copy(k).wait_send()

    @pl.when(is_half)
    def _():
        for k in range(1, nx):
            src_copy(k).wait_send()
        for k in range(nx):
            col_copy(k, half_level, second, row).wait_send()

        @pl.when(level < wide - 1)
        def _():
            for k in range(nx):
                half_copy(k, 0, first, row).wait_send()

        @pl.when(level == wide - 1)
        def _():
            for k in range(nx):
                col_copy(k, half_level, first, row).wait_send()

    @pl.when(is_col)
    def _():
        for d in range(2):
            for k in range(1, nx):
                gather_copy(d, k).wait_send()
        for j in range(nx):
            wide_copy(j, wide_level, 0, row).wait_send()

            @pl.when(level < last)
            def _():
                wide_copy(j, wide_level, 1, row).wait_send()

    low_store.wait()
    up_store.wait()
    src_store.wait()


def body(n, nx, lower_coupling, upper_coupling, solution, cotangent):
    _, half, block = lower_coupling.shape
    width = cotangent.shape[2]
    full = width * nx
    levels = n.bit_length() - 1
    wide = min(2, levels - 1)
    dma = pltpu.SemaphoreType.DMA
    return pl.pallas_call(
        functools.partial(kernel, n, nx, wide),
        out_shape=(
            jax.ShapeDtypeStruct(cotangent.shape, BF16),
            jax.ShapeDtypeStruct(lower_coupling.shape, BF16),
            jax.ShapeDtypeStruct(upper_coupling.shape, BF16),
        ),
        in_specs=[pl.BlockSpec(memory_space=pl.ANY)] * 4,
        out_specs=[pl.BlockSpec(memory_space=pl.ANY)] * 3,
        scratch_shapes=[
            pltpu.VMEM((2, nx, half, block), BF16),
            pltpu.VMEM((block, width), BF16),
            pltpu.VMEM((block, width), BF16),
            pltpu.VMEM((width, block), BF16),
            pltpu.VMEM((full, half), BF16),
            pltpu.VMEM((full, half), F32),
            pltpu.VMEM((full, half), BF16),
            pltpu.VMEM((half, full), BF16),
            pltpu.VMEM((nx, full, half), BF16),
            pltpu.VMEM((max(wide - 1, 1), 2, nx, full, half), BF16),
            pltpu.VMEM((width, block), F32),
            pltpu.VMEM((2, nx, width, block), BF16),
            pltpu.VMEM((wide, 2, nx, width, block), BF16),
            pltpu.VMEM((2, nx, width, half), BF16),
            pltpu.VMEM((levels - wide, 2, nx, width, half), BF16),
            pltpu.VMEM((2, nx, block, width), BF16),
            pltpu.VMEM((width, block), BF16),
            pltpu.VMEM((block, width), BF16),
            pltpu.VMEM((2, half, block), BF16),
            dma((4,)), dma((3,)),
            dma((nx,)), dma((nx,)),
            dma((nx,)), dma((max(wide - 1, 1), 2, nx)),
            dma((2, nx)), dma((wide, 2, nx)),
            dma((2, nx)), dma((levels - wide, 2, nx)),
            dma((2, nx)), dma((2, nx)),
            dma((levels, 2)), dma((2,)),
            dma((2, nx)), dma((2, nx)),
            dma((nx,)), dma((nx,)),
        ],
        compiler_params=pltpu.CompilerParams(
            collective_id=0, has_side_effects=True, vmem_limit_bytes=62 * 1024 * 1024),
    )(lower_coupling, upper_coupling, solution, cotangent)


def solution(mesh):
    in_specs = (
        P("rows", "cols", None),
        P("rows", "cols", None),
        P("rows", None, "cols"),
        P("rows", None, "cols"),
    )
    out_specs = (P("rows", None, "cols"), P("rows", "cols", None), P("rows", "cols", None))
    local = functools.partial(body, mesh.shape["rows"], mesh.shape["cols"])
    return jax.shard_map(local, mesh=mesh, in_specs=in_specs, out_specs=out_specs, check_vma=False)
```
